32 devices in a mesh: dp: 8 (over z, core), group: 4 (over y, x).
Axes of the slice: x: 2, y: 2, z: 4, core: 2. Of those that a mesh axis runs over, the one named last changes fastest.
Arguments:
- layer_input: bfloat16 [2048, 8192], P('dp', 'group'), may hold values from -30 to 30
- kv_cotangent: bfloat16 [2048, 2048], P('dp', 'group'), may hold values from -70 to 70
- weight_codes: bfloat16 [2048, 8192], P('dp', 'group'), may hold values from -256 to 256
- block_scales: bfloat16 [2048, 32], P('dp', 'group'), may hold values from 0.00024986267 to 0.0009994507
- master: float32 [2048, 8192], P('dp', 'group'), may hold values from -6 to 6
- moment_one: float32 [2048, 8192], P('dp', 'group'), may hold values from -0.75 to 0.75
- moment_two: float32 [2048, 8192], P('dp', 'group'), may hold values from 0.001 to 0.01
Outputs:
- grad_input: bfloat16 [2048, 8192], P('dp', 'group')
- new_master: float32 [2048, 8192], P('dp', 'group')
- new_moment_one: float32 [2048, 8192], P('dp', 'group')
- new_moment_two: float32 [2048, 8192], P('dp', 'group')
The draws below stay inside these ranges and needn't reach their ends.
All inputs are finite; a program needn't handle non-finite values.
Results may differ from the reference program's by a relative error of at most 0.0049.
Values may be sent and summed in bfloat16 or wider, within the bound.
A program may use at most 128 MiB of HBM per device.

```python
import math
import jax
import jax.numpy as jnp
from jax import lax

D = 8192
BLOCK = 256
CLIP = 2048
TOK_DEV = 256
KV_COLS = 2048
TOKENS = 2048
N_DP = 8


def column_scales(key, number, rise):
    spread = jax.random.uniform(key, (number,), jnp.float32)
    trend = jnp.arange(number, dtype=jnp.float32) / number
    return jnp.exp(2.302585 * spread + rise * trend) / 4.0


def token_signs(base_key):
    flips = jax.random.randint(jax.random.fold_in(base_key, 41), (TOKENS,), 0, 2)
    return 2.0 * flips.astype(jnp.float32) - 1.0


def scaled_field(key, signs, rows_total, cols_total):
    first_key, second_key, third_key = jax.random.split(key, 3)
    common = jnp.clip(jax.random.normal(third_key, (cols_total,), jnp.float32), -2.0, 2.0)
    shared_weight = float(TOKENS) ** (-0.25)
    values = jnp.clip(jax.random.normal(first_key, (rows_total, cols_total), jnp.float32), -4.0, 4.0)
    scales = column_scales(second_key, cols_total, 0.55)
    values = values + shared_weight * signs[:, None] * common[None, :]
    return values * scales[None, :]


def draw_layer_input(key, part):
    signs = token_signs(key)
    field = scaled_field(jax.random.fold_in(key, 17), signs, TOKENS, D)
    return jnp.clip(field, -30.0, 30.0).astype(jnp.bfloat16)


def draw_kv_cotangent(key, part):
    signs = token_signs(key)
    field_key, pair_key = jax.random.split(jax.random.fold_in(key, 29), 2)
    values = scaled_field(field_key, signs, TOKENS, KV_COLS)
    pairing = jax.random.permutation(pair_key, N_DP)
    row_block = jnp.arange(TOKENS) // TOK_DEV
    col_block = jnp.arange(KV_COLS) // (KV_COLS // N_DP)
    boost = jnp.where(pairing[row_block][:, None] == col_block[None, :], 3.0, 1.0)
    return jnp.clip(values * boost, -70.0, 70.0).astype(jnp.bfloat16)


def steps_of(own_key, shape, cuts, low, top_value):
    loudness, own = 1.0, jax.random.fold_in(own_key, 6)
    for position, parts in cuts:
        heights = jnp.exp(jax.random.uniform(jax.random.fold_in(own, position), (parts,), jnp.float32, low / len(cuts), top_value / len(cuts)))
        loudness = loudness * jnp.repeat(heights, shape[position] // parts).reshape([-1 if axis == position else 1 for axis in range(len(shape))])
    return loudness


def bell_draw(stream_key, shape, scale, reach, pieces=(), kind=jnp.bfloat16):
    level = steps_of(stream_key, shape, pieces, -0.22, 0.18) if pieces else 1.0
    array = jax.random.normal(stream_key, shape, jnp.float32) * scale * level
    return jnp.minimum(jnp.maximum(array, -reach), reach).astype(kind)


def setup_inputs(seed: int = 0) -> dict:
    streams_of = jax.random.split(jax.random.key(seed), 8)
    return {
        "layer_input": draw_layer_input(jax.random.fold_in(streams_of[7], 71), 0),
        "kv_cotangent": draw_kv_cotangent(jax.random.fold_in(streams_of[7], 71), 0),
        "weight_codes": bell_draw(streams_of[2], (KV_COLS, D), 40.0, 256.0, ((0, 8), (1, 4))),
        "block_scales": jnp.clip(jnp.exp(math.log(0.0009994507) - 1.3862944 * jax.random.uniform(streams_of[3], (KV_COLS, D // BLOCK), jnp.float32) ** steps_of(streams_of[3], (KV_COLS, D // BLOCK), ((0, 8), (1, 4)), -0.2, 0.2)), 0.00024986267, 0.0009994507).astype(jnp.bfloat16),
        "master": bell_draw(streams_of[4], (KV_COLS, D), 0.5, 6.0, ((0, 8), (1, 4)), jnp.float32),
        "moment_one": bell_draw(streams_of[5], (KV_COLS, D), 0.05, 0.75, ((0, 8), (1, 4)), jnp.float32),
        "moment_two": jnp.clip(jnp.exp(math.log(0.01) - 2.30258502 * jax.random.uniform(streams_of[6], (KV_COLS, D), jnp.float32) ** steps_of(streams_of[6], (KV_COLS, D), ((0, 8), (1, 4)), -0.2, 0.2)), 0.001, 0.01),
    }


BETA_ONE = 0.9
BETA_TWO = 0.95
LEARN_RATE = 0.25
DECAY_RATE = 0.1
EPS_ADAM = 1e-08
EPS_NORM = 1e-06

def reference(layer_input, kv_cotangent, weight_codes, block_scales, master, moment_one, moment_two):
    blocked = weight_codes.astype(jnp.float32).reshape(KV_COLS, D // BLOCK, BLOCK) * block_scales.astype(jnp.float32)[:, :, None]
    weight = blocked.reshape(KV_COLS, D).astype(jnp.bfloat16)
    grad_input = jnp.dot(kv_cotangent, weight, preferred_element_type=jnp.float32).astype(jnp.bfloat16)
    input_runs = layer_input.reshape(N_DP, TOK_DEV, D)
    cot_runs = kv_cotangent.reshape(N_DP, TOK_DEV, KV_COLS)

    def accumulate(running, pair):
        partial_value = jnp.dot(pair[1].T, pair[0], preferred_element_type=jnp.float32)
        rounded = lax.optimization_barrier(partial_value.astype(jnp.bfloat16))
        return (running + rounded.astype(jnp.float32), None)
    gradient, _ = lax.scan(accumulate, jnp.zeros((KV_COLS, D), jnp.float32), (input_runs, cot_runs))
    norm_value = jnp.sqrt(jnp.sum(gradient * gradient))
    factor = jnp.minimum(1.0, CLIP / (norm_value + EPS_NORM))
    clipped = gradient * factor
    new_moment_one = BETA_ONE * moment_one + (1.0 - BETA_ONE) * clipped
    new_moment_two = BETA_TWO * moment_two + (1.0 - BETA_TWO) * clipped * clipped
    first_fix = 1.0 - BETA_ONE ** 10
    second_fix = 1.0 - BETA_TWO ** 10
    update = new_moment_one / first_fix / (jnp.sqrt(new_moment_two / second_fix) + EPS_ADAM)
    new_master = master - LEARN_RATE * (update + DECAY_RATE * master)
    return (grad_input, new_master, new_moment_one, new_moment_two)
```

```python
import functools
import jax
import jax.numpy as jnp
from jax import lax
from jax.experimental import pallas as pl
from jax.experimental.pallas import tpu as pltpu
from jax.sharding import PartitionSpec as P

BLOCK = 256
CLIP = 2048


BETA_ONE = 0.9
BETA_TWO = 0.95
LEARN_RATE = 0.25
DECAY_RATE = 0.1
EPS_ADAM = 1e-08
EPS_NORM = 1e-06

MESH = pl.DeviceIdType.MESH
PIECES = 4


def dequantize(codes, scales):
    row_count, col_count = codes.shape
    blocked = (
        codes.astype(jnp.float32).reshape(row_count, col_count // BLOCK, BLOCK)
        * scales.astype(jnp.float32)[:, :, None]
    )
    return blocked.reshape(row_count, col_count).astype(jnp.bfloat16)


def adamw(clipped, master, moment_one, moment_two):
    new_moment_one = BETA_ONE * moment_one + (1.0 - BETA_ONE) * clipped
    new_moment_two = BETA_TWO * moment_two + (1.0 - BETA_TWO) * clipped * clipped
    first_fix = 1.0 - BETA_ONE**10
    second_fix = 1.0 - BETA_TWO**10
    update = new_moment_one / first_fix / (jnp.sqrt(new_moment_two / second_fix) + EPS_ADAM)
    new_master = master - LEARN_RATE * (update + DECAY_RATE * master)
    return new_master, new_moment_one, new_moment_two


def general(layer_input, kv_cotangent, weight_codes, block_scales, master, moment_one, moment_two):
    cot_whole = lax.all_gather(kv_cotangent, "group", axis=1, tiled=True)
    weight_piece = dequantize(
        lax.all_gather(weight_codes, "dp", axis=0, tiled=True),
        lax.all_gather(block_scales, "dp", axis=0, tiled=True),
    )
    grad_input = jnp.dot(
        cot_whole, weight_piece, preferred_element_type=jnp.float32
    ).astype(jnp.bfloat16)
    partial_value = jnp.einsum(
        "tc,td->cd", cot_whole, layer_input, preferred_element_type=jnp.float32
    )
    gradient = lax.psum_scatter(
        lax.optimization_barrier(partial_value.astype(jnp.bfloat16)).astype(jnp.float32),
        "dp",
        scatter_dimension=0,
        tiled=True,
    )
    square_total = lax.psum(jnp.sum(gradient * gradient), ("dp", "group"))
    factor = jnp.minimum(1.0, CLIP / (jnp.sqrt(square_total) + EPS_NORM))
    return (grad_input,) + adamw(gradient * factor, master, moment_one, moment_two)


def kernel(
    Z, G, cot_ref, li_ref, codes_ref, scales_ref, gi_ref, g_ref,
    cotp, lip, wbuf, rbuf, facc, gsib, near, far,
    line_send, line_recv, sib_send, sib_recv, cot_send, cot_recv, csib_send, csib_recv,
    li_send, li_recv, fin_send, fin_recv, near_send, near_recv, far_send, far_recv,
):
    K = PIECES
    tok, head = cot_ref.shape
    feat, cols = codes_ref.shape
    half = cols // 2
    unit = 2 * feat
    g_rows, r_rows = feat // K, unit // K

    dp, g = lax.axis_index("dp"), lax.axis_index("group")
    z = lax.div(dp, 2)
    c = dp - 2 * z
    sibling = (2 * z + 1 - c, g)

    def plane(j):
        place = lax.rem(c * G + g + j, 2 * G)
        core = lax.div(place, G)
        return (2 * z + core, place - core * G)

    def line(j):
        return (2 * lax.rem(z + j, Z) + c, g)

    barrier = pltpu.get_barrier_semaphore()
    for j in range(1, 2 * G):
        pl.semaphore_signal(barrier, inc=1, device_id=plane(j), device_id_type=MESH)
    for j in range(1, Z):
        pl.semaphore_signal(barrier, inc=1, device_id=line(j), device_id_type=MESH)
    pl.semaphore_wait(barrier, 2 * G - 1 + Z - 1)

    def remote(src, dst, send, recv, device):
        return pltpu.make_async_remote_copy(
            src_ref=src, dst_ref=dst, send_sem=send, recv_sem=recv,
            device_id=device, device_id_type=MESH,
        )

    def cot_block(owner, core):
        return cotp.at[
            pl.ds(pl.multiple_of(core * tok, tok), tok),
            pl.ds(pl.multiple_of(owner * head, head), head),
        ]

    def cot_copy(j, owner):
        return remote(cot_ref, cot_block(owner, c), cot_send.at[j - 1], cot_recv.at[j - 1],
                      (dp, lax.rem(g + j, G)))

    def cot_pass(j, core):
        owner = lax.rem(g + G - j, G)
        block = cot_block(owner, core)
        return remote(cot_ref if j == 0 else block, block, csib_send.at[j], csib_recv.at[j], sibling)

    for j in range(1, G):
        cot_copy(j, g).start()
    cot_pass(0, c).start()

    def li_copy(core, side):
        return remote(
            li_ref.at[:, pl.ds(pl.multiple_of(side * half, half), half)],
            lip.at[pl.ds(pl.multiple_of(core * tok, tok), tok), :],
            li_send.at[0], li_recv.at[0], sibling,
        )

    li_copy(c, 1 - c).start()

    own = pl.multiple_of(dp * feat, feat)
    for j in range(cols // BLOCK):
        wbuf[pl.ds(own, feat), j * BLOCK:(j + 1) * BLOCK] = (
            codes_ref[:, j * BLOCK:(j + 1) * BLOCK].astype(jnp.float32)
            * scales_ref[:, j:j + 1].astype(jnp.float32)
        ).astype(jnp.bfloat16)

    places = (z, Z - 1 - z)
    nexts = ((dp + 2, g), (dp - 2, g))

    def true_z(way, q):
        return q if way == 0 else Z - 1 - q

    def weight_chunk(zz, core, k):
        return wbuf.at[pl.ds(pl.multiple_of((2 * zz + core) * feat + k * g_rows, g_rows), g_rows), :]

    def sum_chunk(way, dm, k):
        return rbuf.at[way, dm - 1, pl.ds(pl.multiple_of(k * r_rows, r_rows), r_rows), :]

    def line_copy(way, ref, step):
        return remote(ref, ref, line_send.at[way, step], line_recv.at[way, step], nexts[way])

    def sib_copy(zz, core, k):
        ref = weight_chunk(zz, core, k)
        return remote(ref, ref, sib_send.at[zz * K + k], sib_recv.at[zz * K + k], sibling)

    def partial_sum(zz, k):
        first = pl.multiple_of(zz * unit + k * r_rows, r_rows)
        return lax.dot_general(
            cotp[:, pl.ds(first, r_rows)], lip[...],
            (((0,), (0,)), ((), ())), preferred_element_type=jnp.float32,
        )

    def send(way, ref, step):
        @pl.when(step >= 2)
        def _():
            line_copy(way, weight_chunk(z, c, 0), step - 2).wait_send()
        line_copy(way, ref, step).start()

    def weight_step(way, s, k):
        p = places[way]

        @pl.when(s <= p)
        def _():
            zz = true_z(way, p - s)
            ref = weight_chunk(zz, c, k)

            @pl.when(s > 0)
            def _():
                line_copy(way, ref, (s - 1) * K + k).wait_recv()

            @pl.when((s > 0) if way else (s >= 0))
            def _():
                sib_copy(zz, c, k).start()

            @pl.when(p < Z - 1)
            def _():
                send(way, ref, s * K + k)

    def sum_step(way, s, k):
        p = places[way]

        @pl.when((s > p) & (p < Z - 1))
        def _():
            dm = Z + p - s
            ref = sum_chunk(way, dm, k)
            value = partial_sum(true_z(way, dm), k)

            @pl.when(p > 0)
            def _():
                line_copy(way, ref, (s - 1) * K + k).wait_recv()
                ref[...] = (ref[...].astype(jnp.float32) + value).astype(jnp.bfloat16)

            @pl.when(p == 0)
            def _():
                ref[...] = value.astype(jnp.bfloat16)

            send(way, ref, s * K + k)

    def first_unit(k, carry):
        for way in (0, 1):
            weight_step(way, 0, k)
        return carry

    lax.fori_loop(0, 2, first_unit, 0)
    lip[pl.ds(pl.multiple_of(c * tok, tok), tok), :] = li_ref[
        :, pl.ds(pl.multiple_of(c * half, half), half)]
    cotp[pl.ds(pl.multiple_of(c * tok, tok), tok), pl.ds(pl.multiple_of(g * head, head), head)] = cot_ref[...]
    for j in range(1, G):
        cot_copy(j, lax.rem(g + G - j, G)).wait_recv()
        cot_pass(j, c).start()
    lax.fori_loop(2, K, first_unit, 0)
    li_copy(1 - c, c).wait_recv()
    for j in range(G):
        cot_pass(j, 1 - c).wait_recv()

    def later_unit(i, carry):
        s = lax.div(i, K)
        k = i - s * K
        for way in (0, 1):
            weight_step(way, s, k)
        for way in (0, 1):
            sum_step(way, s, k)
        return carry

    lax.fori_loop(K, Z * K, later_unit, 0)

    def arrive(i, carry):
        zz = lax.div(i, K)
        sib_copy(zz, 1 - c, i - zz * K).wait_recv()
        return carry

    lax.fori_loop(0, Z * K, arrive, 0)

    def input_tile(j, carry):
        at = pl.ds(pl.multiple_of(j * BLOCK, BLOCK), BLOCK)
        gi_ref[:, at] = jnp.dot(
            cotp[pl.ds(pl.multiple_of(c * tok, tok), tok), :], wbuf[:, at],
            preferred_element_type=jnp.float32,
        ).astype(jnp.bfloat16)
        return carry

    lax.fori_loop(0, cols // BLOCK, input_tile, 0)

    def own_sum(k, carry):
        facc[pl.ds(pl.multiple_of(k * r_rows, r_rows), r_rows), :] = partial_sum(z, k)
        return carry

    lax.fori_loop(0, K, own_sum, 0)

    def fin_copy(k, m):
        return remote(
            facc.at[pl.ds(pl.multiple_of(k * r_rows, r_rows), r_rows), :],
            gsib.at[pl.ds(pl.multiple_of(m * r_rows, r_rows), r_rows), :],
            fin_send.at[m], fin_recv.at[m], sibling,
        )

    near[0] = jnp.zeros(near.shape[1:], jnp.float32)

    def finish(k, carry):
        at = pl.ds(pl.multiple_of(k * r_rows, r_rows), r_rows)
        for way in (0, 1):
            p = places[way]

            @pl.when(p > 0)
            def _():
                ref = sum_chunk(way, p, k)
                line_copy(way, ref, (Z - 1) * K + k).wait_recv()
                facc[at, :] += ref[...].astype(jnp.float32)

        core = lax.div(k, K // 2)

        @pl.when(core != c)
        def _():
            fin_copy(k, k - core * (K // 2)).start()

        value = facc[at, :]
        squares = value * value
        total = squares[0:8, :]
        for i in range(1, r_rows // 8):
            total = total + squares[i * 8:(i + 1) * 8, :]
        short = total[:, 0:128]
        for i in range(1, half // 128):
            short = short + total[:, i * 128:(i + 1) * 128]
        near[0] += short
        return carry

    lax.fori_loop(0, K, finish, 0)

    for j in range(1, 2 * G):
        remote(near.at[0], near.at[j], near_send.at[j - 1], near_recv.at[j - 1], plane(j)).start()
    for j in range(1, 2 * G):
        remote(near.at[0], near.at[j], near_send.at[j - 1], near_recv.at[j - 1], plane(j)).wait_recv()
    total = near[0]
    for j in range(1, 2 * G):
        total = total + near[j]
    far[0] = total
    for j in range(1, Z):
        remote(far.at[0], far.at[j], far_send.at[j - 1], far_recv.at[j - 1], line(j)).start()
    for j in range(1, Z):
        remote(far.at[0], far.at[j], far_send.at[j - 1], far_recv.at[j - 1], line(j)).wait_recv()
    total = far[0]
    for j in range(1, Z):
        total = total + far[j]
    square_total = jnp.sum(total, axis=(0, 1), keepdims=True)
    factor = jnp.minimum(1.0, CLIP / (jnp.sqrt(square_total) + EPS_NORM))

    g_ref[:, pl.ds(pl.multiple_of(c * half, half), half)] = (
        facc[pl.ds(pl.multiple_of(c * feat, feat), feat), :] * factor)
    for m in range(K // 2):
        fin_copy(m, m).wait_recv()
    g_ref[:, pl.ds(pl.multiple_of((1 - c) * half, half), half)] = gsib[...] * factor

    for j in range(1, G):
        cot_copy(j, g).wait_send()
    for j in range(G):
        cot_pass(j, c).wait_send()
    li_copy(c, 1 - c).wait_send()

    def sent(i, carry):
        zz = lax.div(i, K)
        sib_copy(zz, c, i - zz * K).wait_send()
        return carry

    lax.fori_loop(0, Z * K, sent, 0)
    for way in (0, 1):
        @pl.when(places[way] < Z - 1)
        def _():
            for step in (Z * K - 2, Z * K - 1):
                line_copy(way, weight_chunk(z, c, 0), step).wait_send()
    for m in range(K // 2):
        fin_copy(m, m).wait_send()
    for j in range(1, 2 * G):
        remote(near.at[0], near.at[j], near_send.at[j - 1], near_recv.at[j - 1], plane(j)).wait_send()
    for j in range(1, Z):
        remote(far.at[0], far.at[j], far_send.at[j - 1], far_recv.at[j - 1], line(j)).wait_send()


def fused(Z, G, layer_input, kv_cotangent, weight_codes, block_scales, master, moment_one, moment_two):
    tok, head = kv_cotangent.shape
    feat, cols = weight_codes.shape
    half = cols // 2
    K = PIECES
    dma = pltpu.SemaphoreType.DMA
    vmem = pl.BlockSpec(memory_space=pltpu.VMEM)
    grad_input, clipped = pl.pallas_call(
        functools.partial(kernel, Z, G),
        out_shape=(
            jax.ShapeDtypeStruct((tok, cols), jnp.bfloat16),
            jax.ShapeDtypeStruct((feat, cols), jnp.float32),
        ),
        in_specs=[vmem] * 4,
        out_specs=(vmem, vmem),
        scratch_shapes=[
            pltpu.VMEM((2 * tok, G * head), jnp.bfloat16),
            pltpu.VMEM((2 * tok, half), jnp.bfloat16),
            pltpu.VMEM((2 * Z * feat, cols), jnp.bfloat16),
            pltpu.VMEM((2, Z - 1, 2 * feat, half), jnp.bfloat16),
            pltpu.VMEM((2 * feat, half), jnp.float32),
            pltpu.VMEM((feat, half), jnp.float32),
            pltpu.VMEM((2 * G, 8, 128), jnp.float32),
            pltpu.VMEM((Z, 8, 128), jnp.float32),
            dma((2, Z * K)), dma((2, Z * K)),
            dma((Z * K,)), dma((Z * K,)),
            dma((G - 1,)), dma((G - 1,)),
            dma((G,)), dma((G,)),
            dma((1,)), dma((1,)),
            dma((K // 2,)), dma((K // 2,)),
            dma((2 * G - 1,)), dma((2 * G - 1,)),
            dma((Z - 1,)), dma((Z - 1,)),
        ],
        compiler_params=pltpu.CompilerParams(
            collective_id=0, has_side_effects=True, vmem_limit_bytes=48 * 1024 * 1024,
        ),
        cost_estimate=pl.CostEstimate(
            flops=4 * tok * G * head * cols, bytes_accessed=10 * tok * cols, transcendentals=0,
        ),
    )(kv_cotangent, layer_input, weight_codes, block_scales)
    return (grad_input,) + adamw(clipped, master, moment_one, moment_two)


def solution(mesh):
    devices, groups = mesh.shape["dp"], mesh.shape["group"]

    def shards(*args):
        tok, head = args[1].shape
        feat, cols = args[2].shape
        if devices == 8 and groups == 4 and feat == 256 and tok == 256 and cols % 512 == 0 and head == 2 * feat:
            return fused(devices // 2, groups, *args)
        return general(*args)

    return jax.shard_map(
        shards,
        mesh=mesh,
        in_specs=(P("dp", "group"),) * 7,
        out_specs=(P("dp", "group"), P("dp", "group"), P("dp", "group"), P("dp", "group")),
        check_vma=False,
    )
```

```python
import functools
import jax
import jax.numpy as jnp
from jax import lax
from jax.experimental import pallas as pl
from jax.experimental.pallas import tpu as pltpu
from jax.sharding import PartitionSpec as P

BLOCK = 256
CLIP = 2048


BETA_ONE = 0.9
BETA_TWO = 0.95
LEARN_RATE = 0.25
DECAY_RATE = 0.1
EPS_ADAM = 1e-08
EPS_NORM = 1e-06

MESH = pl.DeviceIdType.MESH
PIECES = 4
DEPTH = 3


def dequantize(codes, scales):
    row_count, col_count = codes.shape
    blocked = (
        codes.astype(jnp.float32).reshape(row_count, col_count // BLOCK, BLOCK)
        * scales.astype(jnp.float32)[:, :, None]
    )
    return blocked.reshape(row_count, col_count).astype(jnp.bfloat16)


def adamw(clipped, master, moment_one, moment_two):
    new_moment_one = BETA_ONE * moment_one + (1.0 - BETA_ONE) * clipped
    new_moment_two = BETA_TWO * moment_two + (1.0 - BETA_TWO) * clipped * clipped
    first_fix = 1.0 - BETA_ONE**10
    second_fix = 1.0 - BETA_TWO**10
    update = new_moment_one / first_fix / (jnp.sqrt(new_moment_two / second_fix) + EPS_ADAM)
    new_master = master - LEARN_RATE * (update + DECAY_RATE * master)
    return new_master, new_moment_one, new_moment_two


def general(layer_input, kv_cotangent, weight_codes, block_scales, master, moment_one, moment_two):
    cot_whole = lax.all_gather(kv_cotangent, "group", axis=1, tiled=True)
    weight_piece = dequantize(
        lax.all_gather(weight_codes, "dp", axis=0, tiled=True),
        lax.all_gather(block_scales, "dp", axis=0, tiled=True),
    )
    grad_input = jnp.dot(
        cot_whole, weight_piece, preferred_element_type=jnp.float32
    ).astype(jnp.bfloat16)
    partial_value = jnp.einsum(
        "tc,td->cd", cot_whole, layer_input, preferred_element_type=jnp.float32
    )
    gradient = lax.psum_scatter(
        lax.optimization_barrier(partial_value.astype(jnp.bfloat16)).astype(jnp.float32),
        "dp",
        scatter_dimension=0,
        tiled=True,
    )
    square_total = lax.psum(jnp.sum(gradient * gradient), ("dp", "group"))
    factor = jnp.minimum(1.0, CLIP / (jnp.sqrt(square_total) + EPS_NORM))
    return (grad_input,) + adamw(gradient * factor, master, moment_one, moment_two)


def kernel(
    Z, G, cot_ref, li_ref, codes_ref, scales_ref, gi_ref, g_ref,
    cotp, lip, wbuf, rbuf, facc, gsib, near, far, local,
    line_send, line_recv, sib_send, sib_recv, cot_send, cot_recv, csib_send, csib_recv,
    li_send, li_recv, fin_send, fin_recv, near_send, near_recv, far_send, far_recv,
):
    K = PIECES
    tok, head = cot_ref.shape
    feat, cols = codes_ref.shape
    half = cols // 2
    unit = 2 * feat
    g_rows, r_rows = feat // K, unit // K

    dp, g = lax.axis_index("dp"), lax.axis_index("group")
    z = lax.div(dp, 2)
    c = dp - 2 * z
    sibling = (2 * z + 1 - c, g)

    def plane(j):
        place = lax.rem(c * G + g + j, 2 * G)
        core = lax.div(place, G)
        return (2 * z + core, place - core * G)

    def line(j):
        return (2 * lax.rem(z + j, Z) + c, g)

    barrier = pltpu.get_barrier_semaphore()
    for j in range(1, 2 * G):
        pl.semaphore_signal(barrier, inc=1, device_id=plane(j), device_id_type=MESH)
    for j in range(1, Z):
        pl.semaphore_signal(barrier, inc=1, device_id=line(j), device_id_type=MESH)

    own_tok = pl.ds(pl.multiple_of(c * tok, tok), tok)
    fetch_li = pltpu.make_async_copy(
        li_ref.at[:, pl.ds(pl.multiple_of(c * half, half), half)], lip.at[own_tok, :], local.at[0])
    fetch_cot = pltpu.make_async_copy(
        cot_ref, cotp.at[own_tok, pl.ds(pl.multiple_of(g * head, head), head)], local.at[1])
    fetch_li.start()
    fetch_cot.start()

    own = pl.multiple_of(dp * feat, feat)
    scales = scales_ref[...].astype(jnp.float32).T
    for j in range(cols // BLOCK):
        wbuf[pl.ds(own, feat), j * BLOCK:(j + 1) * BLOCK] = (
            codes_ref[:, j * BLOCK:(j + 1) * BLOCK].astype(jnp.float32) * scales[:, j:j + 1]
        ).astype(jnp.bfloat16)

    pl.semaphore_wait(barrier, 2 * G - 1 + Z - 1)

    def remote(src, dst, send, recv, device):
        return pltpu.make_async_remote_copy(
            src_ref=src, dst_ref=dst, send_sem=send, recv_sem=recv,
            device_id=device, device_id_type=MESH,
        )

    def cot_block(owner, core):
        return cotp.at[
            pl.ds(pl.multiple_of(core * tok, tok), tok),
            pl.ds(pl.multiple_of(owner * head, head), head),
        ]

    def cot_copy(j, owner):
        return remote(cot_ref, cot_block(owner, c), cot_send.at[j - 1], cot_recv.at[j - 1],
                      (dp, lax.rem(g + j, G)))

    def cot_pass(j, core):
        owner = lax.rem(g + G - j, G)
        block = cot_block(owner, core)
        return remote(cot_ref if j == 0 else block, block, csib_send.at[j], csib_recv.at[j], sibling)

    for j in range(1, G):
        cot_copy(j, g).start()
    cot_pass(0, c).start()

    def li_copy(core, side):
        return remote(
            li_ref.at[:, pl.ds(pl.multiple_of(side * half, half), half)],
            lip.at[pl.ds(pl.multiple_of(core * tok, tok), tok), :],
            li_send.at[0], li_recv.at[0], sibling,
        )

    li_copy(c, 1 - c).start()

    places = (z, Z - 1 - z)
    nexts = ((dp + 2, g), (dp - 2, g))

    def true_z(way, q):
        return q if way == 0 else Z - 1 - q

    def weight_chunk(zz, core, k):
        return wbuf.at[pl.ds(pl.multiple_of((2 * zz + core) * feat + k * g_rows, g_rows), g_rows), :]

    def sum_chunk(way, dm, k):
        return rbuf.at[way, dm - 1, pl.ds(pl.multiple_of(k * r_rows, r_rows), r_rows), :]

    def line_copy(way, ref, step):
        return remote(ref, ref, line_send.at[way, step], line_recv.at[way, step], nexts[way])

    def sib_copy(zz, core, k):
        ref = weight_chunk(zz, core, k)
        return remote(ref, ref, sib_send.at[zz * K + k], sib_recv.at[zz * K + k], sibling)

    def partial_sum(zz, k):
        first = pl.multiple_of(zz * unit + k * r_rows, r_rows)
        return lax.dot_general(
            cotp[:, pl.ds(first, r_rows)], lip[...],
            (((0,), (0,)), ((), ())), preferred_element_type=jnp.float32,
        )

    def send(way, ref, step):
        @pl.when(step >= DEPTH)
        def _():
            line_copy(way, weight_chunk(z, c, 0), step - DEPTH).wait_send()
        line_copy(way, ref, step).start()

    def weight_step(way, s, k):
        p = places[way]

        @pl.when(s <= p)
        def _():
            zz = true_z(way, p - s)
            ref = weight_chunk(zz, c, k)

            @pl.when(s > 0)
            def _():
                line_copy(way, ref, (s - 1) * K + k).wait_recv()

            @pl.when((s > 0) if way else (s >= 0))
            def _():
                sib_copy(zz, c, k).start()

            @pl.when(p < Z - 1)
            def _():
                send(way, ref, s * K + k)

    def sum_step(way, s, k):
        p = places[way]

        @pl.when((s > p) & (p < Z - 1))
        def _():
            dm = Z + p - s
            ref = sum_chunk(way, dm, k)
            value = partial_sum(true_z(way, dm), k)

            @pl.when(p > 0)
            def _():
                line_copy(way, ref, (s - 1) * K + k).wait_recv()
                ref[...] = (ref[...].astype(jnp.float32) + value).astype(jnp.bfloat16)

            @pl.when(p == 0)
            def _():
                ref[...] = value.astype(jnp.bfloat16)

            send(way, ref, s * K + k)

    def first_unit(k, carry):
        for way in (0, 1):
            weight_step(way, 0, k)
        return carry

    lax.fori_loop(0, DEPTH, first_unit, 0)
    for j in range(1, G):
        cot_copy(j, lax.rem(g + G - j, G)).wait_recv()
        cot_pass(j, c).start()
    lax.fori_loop(DEPTH, K, first_unit, 0)
    fetch_li.wait()
    fetch_cot.wait()
    li_copy(1 - c, c).wait_recv()
    for j in range(G):
        cot_pass(j, 1 - c).wait_recv()

    def later_unit(i, carry):
        s = lax.div(i, K)
        k = i - s * K
        for way in (0, 1):
            weight_step(way, s, k)
        for way in (0, 1):
            sum_step(way, s, k)
        return carry

    lax.fori_loop(K, Z * K, later_unit, 0)

    def arrive(i, carry):
        zz = lax.div(i, K)
        sib_copy(zz, 1 - c, i - zz * K).wait_recv()
        return carry

    lax.fori_loop(0, Z * K, arrive, 0)

    def input_tile(j, carry):
        at = pl.ds(pl.multiple_of(j * BLOCK, BLOCK), BLOCK)
        gi_ref[:, at] = jnp.dot(
            cotp[pl.ds(pl.multiple_of(c * tok, tok), tok), :], wbuf[:, at],
            preferred_element_type=jnp.float32,
        ).astype(jnp.bfloat16)
        return carry

    lax.fori_loop(0, cols // BLOCK, input_tile, 0)

    def own_sum(k, carry):
        facc[pl.ds(pl.multiple_of(k * r_rows, r_rows), r_rows), :] = partial_sum(z, k)
        return carry

    lax.fori_loop(0, K, own_sum, 0)

    def fin_copy(k, m):
        return remote(
            facc.at[pl.ds(pl.multiple_of(k * r_rows, r_rows), r_rows), :],
            gsib.at[pl.ds(pl.multiple_of(m * r_rows, r_rows), r_rows), :],
            fin_send.at[m], fin_recv.at[m], sibling,
        )

    near[0] = jnp.zeros(near.shape[1:], jnp.float32)

    def finish(k, carry):
        at = pl.ds(pl.multiple_of(k * r_rows, r_rows), r_rows)
        for way in (0, 1):
            p = places[way]

            @pl.when(p > 0)
            def _():
                ref = sum_chunk(way, p, k)
                line_copy(way, ref, (Z - 1) * K + k).wait_recv()
                facc[at, :] += ref[...].astype(jnp.float32)

        core = lax.div(k, K // 2)

        @pl.when(core != c)
        def _():
            fin_copy(k, k - core * (K // 2)).start()

        value = facc[at, :]
        squares = value * value
        total = squares[0:8, :]
        for i in range(1, r_rows // 8):
            total = total + squares[i * 8:(i + 1) * 8, :]
        short = total[:, 0:128]
        for i in range(1, half // 128):
            short = short + total[:, i * 128:(i + 1) * 128]
        near[0] += short
        return carry

    lax.fori_loop(0, K, finish, 0)

    for j in range(1, 2 * G):
        remote(near.at[0], near.at[j], near_send.at[j - 1], near_recv.at[j - 1], plane(j)).start()
    for j in range(1, 2 * G):
        remote(near.at[0], near.at[j], near_send.at[j - 1], near_recv.at[j - 1], plane(j)).wait_recv()
    total = near[0]
    for j in range(1, 2 * G):
        total = total + near[j]
    far[0] = total
    for j in range(1, Z):
        remote(far.at[0], far.at[j], far_send.at[j - 1], far_recv.at[j - 1], line(j)).start()
    for j in range(1, Z):
        remote(far.at[0], far.at[j], far_send.at[j - 1], far_recv.at[j - 1], line(j)).wait_recv()
    total = far[0]
    for j in range(1, Z):
        total = total + far[j]
    square_total = jnp.sum(total, axis=(0, 1), keepdims=True)
    factor = jnp.minimum(1.0, CLIP / (jnp.sqrt(square_total) + EPS_NORM))

    g_ref[:, pl.ds(pl.multiple_of(c * half, half), half)] = (
        facc[pl.ds(pl.multiple_of(c * feat, feat), feat), :] * factor)
    for m in range(K // 2):
        fin_copy(m, m).wait_recv()
    g_ref[:, pl.ds(pl.multiple_of((1 - c) * half, half), half)] = gsib[...] * factor

    for j in range(1, G):
        cot_copy(j, g).wait_send()
    for j in range(G):
        cot_pass(j, c).wait_send()
    li_copy(c, 1 - c).wait_send()

    def sent(i, carry):
        zz = lax.div(i, K)
        sib_copy(zz, c, i - zz * K).wait_send()
        return carry

    lax.fori_loop(0, Z * K, sent, 0)
    for way in (0, 1):
        @pl.when(places[way] < Z - 1)
        def _():
            for step in range(Z * K - DEPTH, Z * K):
                line_copy(way, weight_chunk(z, c, 0), step).wait_send()
    for m in range(K // 2):
        fin_copy(m, m).wait_send()
    for j in range(1, 2 * G):
        remote(near.at[0], near.at[j], near_send.at[j - 1], near_recv.at[j - 1], plane(j)).wait_send()
    for j in range(1, Z):
        remote(far.at[0], far.at[j], far_send.at[j - 1], far_recv.at[j - 1], line(j)).wait_send()


def fused(Z, G, layer_input, kv_cotangent, weight_codes, block_scales, master, moment_one, moment_two):
    tok, head = kv_cotangent.shape
    feat, cols = weight_codes.shape
    half = cols // 2
    K = PIECES
    dma = pltpu.SemaphoreType.DMA
    vmem = pl.BlockSpec(memory_space=pltpu.VMEM)
    whole = pl.BlockSpec(memory_space=pltpu.HBM)
    grad_input, clipped = pl.pallas_call(
        functools.partial(kernel, Z, G),
        out_shape=(
            jax.ShapeDtypeStruct((tok, cols), jnp.bfloat16),
            jax.ShapeDtypeStruct((feat, cols), jnp.float32),
        ),
        in_specs=[whole, whole, vmem, vmem],
        out_specs=(vmem, vmem),
        scratch_shapes=[
            pltpu.VMEM((2 * tok, G * head), jnp.bfloat16),
            pltpu.VMEM((2 * tok, half), jnp.bfloat16),
            pltpu.VMEM((2 * Z * feat, cols), jnp.bfloat16),
            pltpu.VMEM((2, Z - 1, 2 * feat, half), jnp.bfloat16),
            pltpu.VMEM((2 * feat, half), jnp.float32),
            pltpu.VMEM((feat, half), jnp.float32),
            pltpu.VMEM((2 * G, 8, 128), jnp.float32),
            pltpu.VMEM((Z, 8, 128), jnp.float32),
            dma((2,)),
            dma((2, Z * K)), dma((2, Z * K)),
            dma((Z * K,)), dma((Z * K,)),
            dma((G - 1,)), dma((G - 1,)),
            dma((G,)), dma((G,)),
            dma((1,)), dma((1,)),
            dma((K // 2,)), dma((K // 2,)),
            dma((2 * G - 1,)), dma((2 * G - 1,)),
            dma((Z - 1,)), dma((Z - 1,)),
        ],
        compiler_params=pltpu.CompilerParams(
            collective_id=0, has_side_effects=True, vmem_limit_bytes=48 * 1024 * 1024,
        ),
        cost_estimate=pl.CostEstimate(
            flops=4 * tok * G * head * cols, bytes_accessed=10 * tok * cols, transcendentals=0,
        ),
    )(kv_cotangent, layer_input, weight_codes, block_scales.T)
    return (grad_input,) + adamw(clipped, master, moment_one, moment_two)


def solution(mesh):
    devices, groups = mesh.shape["dp"], mesh.shape["group"]

    def shards(*args):
        tok, head = args[1].shape
        feat, cols = args[2].shape
        if devices == 8 and groups == 4 and feat == 256 and tok == 256 and cols % 512 == 0 and head == 2 * feat:
            return fused(devices // 2, groups, *args)
        return general(*args)

    return jax.shard_map(
        shards,
        mesh=mesh,
        in_specs=(P("dp", "group"),) * 7,
        out_specs=(P("dp", "group"), P("dp", "group"), P("dp", "group"), P("dp", "group")),
        check_vma=False,
    )
```

```python
import functools
import jax
import jax.numpy as jnp
from jax import lax
from jax.experimental import pallas as pl
from jax.experimental.pallas import tpu as pltpu
from jax.sharding import PartitionSpec as P

BLOCK = 256
CLIP = 2048


BETA_ONE = 0.9
BETA_TWO = 0.95
LEARN_RATE = 0.25
DECAY_RATE = 0.1
EPS_ADAM = 1e-08
EPS_NORM = 1e-06

MESH = pl.DeviceIdType.MESH
PIECES = 4
DEPTH = 3


def dequantize(codes, scales):
    row_count, col_count = codes.shape
    blocked = (
        codes.astype(jnp.float32).reshape(row_count, col_count // BLOCK, BLOCK)
        * scales.astype(jnp.float32)[:, :, None]
    )
    return blocked.reshape(row_count, col_count).astype(jnp.bfloat16)


def adamw(clipped, master, moment_one, moment_two):
    new_moment_one = BETA_ONE * moment_one + (1.0 - BETA_ONE) * clipped
    new_moment_two = BETA_TWO * moment_two + (1.0 - BETA_TWO) * clipped * clipped
    first_fix = 1.0 - BETA_ONE**10
    second_fix = 1.0 - BETA_TWO**10
    update = new_moment_one / first_fix / (jnp.sqrt(new_moment_two / second_fix) + EPS_ADAM)
    new_master = master - LEARN_RATE * (update + DECAY_RATE * master)
    return new_master, new_moment_one, new_moment_two


def general(layer_input, kv_cotangent, weight_codes, block_scales, master, moment_one, moment_two):
    cot_whole = lax.all_gather(kv_cotangent, "group", axis=1, tiled=True)
    weight_piece = dequantize(
        lax.all_gather(weight_codes, "dp", axis=0, tiled=True),
        lax.all_gather(block_scales, "dp", axis=0, tiled=True),
    )
    grad_input = jnp.dot(
        cot_whole, weight_piece, preferred_element_type=jnp.float32
    ).astype(jnp.bfloat16)
    partial_value = jnp.einsum(
        "tc,td->cd", cot_whole, layer_input, preferred_element_type=jnp.float32
    )
    gradient = lax.psum_scatter(
        lax.optimization_barrier(partial_value.astype(jnp.bfloat16)).astype(jnp.float32),
        "dp",
        scatter_dimension=0,
        tiled=True,
    )
    square_total = lax.psum(jnp.sum(gradient * gradient), ("dp", "group"))
    factor = jnp.minimum(1.0, CLIP / (jnp.sqrt(square_total) + EPS_NORM))
    return (grad_input,) + adamw(gradient * factor, master, moment_one, moment_two)


def kernel(
    Z, G, cot_ref, li_ref, codes_ref, scales_ref, gi_ref, g_ref,
    codes, scales_in, cotp, lip, wbuf, rbuf, facc, gsib, near, far, local,
    line_send, line_recv, sib_send, sib_recv, cot_send, cot_recv, csib_send, csib_recv,
    li_send, li_recv, fin_send, fin_recv, near_send, near_recv, far_send, far_recv,
):
    K = PIECES
    tok, head = cot_ref.shape
    feat, cols = codes_ref.shape
    half = cols // 2
    unit = 2 * feat
    g_rows, r_rows = feat // K, unit // K

    dp, g = lax.axis_index("dp"), lax.axis_index("group")
    z = lax.div(dp, 2)
    c = dp - 2 * z
    sibling = (2 * z + 1 - c, g)

    def plane(j):
        place = lax.rem(c * G + g + j, 2 * G)
        core = lax.div(place, G)
        return (2 * z + core, place - core * G)

    def line(j):
        return (2 * lax.rem(z + j, Z) + c, g)

    barrier = pltpu.get_barrier_semaphore()
    for j in range(1, 2 * G):
        pl.semaphore_signal(barrier, inc=1, device_id=plane(j), device_id_type=MESH)
    for j in range(1, Z):
        pl.semaphore_signal(barrier, inc=1, device_id=line(j), device_id_type=MESH)

    fetch_codes = pltpu.make_async_copy(codes_ref, codes, local.at[2])
    fetch_scales = pltpu.make_async_copy(scales_ref, scales_in, local.at[3])
    fetch_codes.start()
    fetch_scales.start()
    own_tok = pl.ds(pl.multiple_of(c * tok, tok), tok)
    fetch_li = pltpu.make_async_copy(
        li_ref.at[:, pl.ds(pl.multiple_of(c * half, half), half)], lip.at[own_tok, :], local.at[0])
    fetch_cot = pltpu.make_async_copy(
        cot_ref, cotp.at[own_tok, pl.ds(pl.multiple_of(g * head, head), head)], local.at[1])
    fetch_li.start()
    fetch_cot.start()

    own = pl.multiple_of(dp * feat, feat)
    fetch_scales.wait()
    scales = scales_in[...].astype(jnp.float32).T
    fetch_codes.wait()
    for j in range(cols // BLOCK):
        wbuf[pl.ds(own, feat), j * BLOCK:(j + 1) * BLOCK] = (
            codes[:, j * BLOCK:(j + 1) * BLOCK].astype(jnp.float32) * scales[:, j:j + 1]
        ).astype(jnp.bfloat16)

    pl.semaphore_wait(barrier, 2 * G - 1 + Z - 1)

    def remote(src, dst, send, recv, device):
        return pltpu.make_async_remote_copy(
            src_ref=src, dst_ref=dst, send_sem=send, recv_sem=recv,
            device_id=device, device_id_type=MESH,
        )

    def cot_block(owner, core):
        return cotp.at[
            pl.ds(pl.multiple_of(core * tok, tok), tok),
            pl.ds(pl.multiple_of(owner * head, head), head),
        ]

    def cot_copy(j, owner):
        return remote(cot_ref, cot_block(owner, c), cot_send.at[j - 1], cot_recv.at[j - 1],
                      (dp, lax.rem(g + j, G)))

    def cot_pass(j, core):
        owner = lax.rem(g + G - j, G)
        block = cot_block(owner, core)
        return remote(cot_ref if j == 0 else block, block, csib_send.at[j], csib_recv.at[j], sibling)

    for j in range(1, G):
        cot_copy(j, g).start()
    cot_pass(0, c).start()

    def li_copy(core, side):
        return remote(
            li_ref.at[:, pl.ds(pl.multiple_of(side * half, half), half)],
            lip.at[pl.ds(pl.multiple_of(core * tok, tok), tok), :],
            li_send.at[0], li_recv.at[0], sibling,
        )

    li_copy(c, 1 - c).start()

    places = (z, Z - 1 - z)
    nexts = ((dp + 2, g), (dp - 2, g))

    def true_z(way, q):
        return q if way == 0 else Z - 1 - q

    def weight_chunk(zz, core, k):
        return wbuf.at[pl.ds(pl.multiple_of((2 * zz + core) * feat + k * g_rows, g_rows), g_rows), :]

    def sum_chunk(way, dm, k):
        return rbuf.at[way, dm - 1, pl.ds(pl.multiple_of(k * r_rows, r_rows), r_rows), :]

    def line_copy(way, ref, step):
        return remote(ref, ref, line_send.at[way, step], line_recv.at[way, step], nexts[way])

    def sib_copy(zz, core, k):
        ref = weight_chunk(zz, core, k)
        return remote(ref, ref, sib_send.at[zz * K + k], sib_recv.at[zz * K + k], sibling)

    def partial_sum(zz, k):
        first = pl.multiple_of(zz * unit + k * r_rows, r_rows)
        return lax.dot_general(
            cotp[:, pl.ds(first, r_rows)], lip[...],
            (((0,), (0,)), ((), ())), preferred_element_type=jnp.float32,
        )

    def send(way, ref, step):
        @pl.when(step >= DEPTH)
        def _():
            line_copy(way, weight_chunk(z, c, 0), step - DEPTH).wait_send()
        line_copy(way, ref, step).start()

    def weight_step(way, s, k):
        p = places[way]

        @pl.when(s <= p)
        def _():
            zz = true_z(way, p - s)
            ref = weight_chunk(zz, c, k)

            @pl.when(s > 0)
            def _():
                line_copy(way, ref, (s - 1) * K + k).wait_recv()

            @pl.when((s > 0) if way else (s >= 0))
            def _():
                sib_copy(zz, c, k).start()

            @pl.when(p < Z - 1)
            def _():
                send(way, ref, s * K + k)

    def sum_step(way, s, k):
        p = places[way]

        @pl.when((s > p) & (p < Z - 1))
        def _():
            dm = Z + p - s
            ref = sum_chunk(way, dm, k)
            value = partial_sum(true_z(way, dm), k)

            @pl.when(p > 0)
            def _():
                line_copy(way, ref, (s - 1) * K + k).wait_recv()
                ref[...] = (ref[...].astype(jnp.float32) + value).astype(jnp.bfloat16)

            @pl.when(p == 0)
            def _():
                ref[...] = value.astype(jnp.bfloat16)

            send(way, ref, s * K + k)

    def first_unit(k, carry):
        for way in (0, 1):
            weight_step(way, 0, k)
        return carry

    lax.fori_loop(0, DEPTH, first_unit, 0)
    for j in range(1, G):
        cot_copy(j, lax.rem(g + G - j, G)).wait_recv()
        cot_pass(j, c).start()
    lax.fori_loop(DEPTH, K, first_unit, 0)
    fetch_li.wait()
    fetch_cot.wait()
    li_copy(1 - c, c).wait_recv()
    for j in range(G):
        cot_pass(j, 1 - c).wait_recv()

    def later_unit(i, carry):
        s = lax.div(i, K)
        k = i - s * K
        for way in (0, 1):
            weight_step(way, s, k)
        for way in (0, 1):
            sum_step(way, s, k)
        return carry

    lax.fori_loop(K, Z * K, later_unit, 0)

    def arrive(i, carry):
        zz = lax.div(i, K)
        sib_copy(zz, 1 - c, i - zz * K).wait_recv()
        return carry

    lax.fori_loop(0, Z * K, arrive, 0)

    def input_tile(j, carry):
        at = pl.ds(pl.multiple_of(j * BLOCK, BLOCK), BLOCK)
        gi_ref[:, at] = jnp.dot(
            cotp[pl.ds(pl.multiple_of(c * tok, tok), tok), :], wbuf[:, at],
            preferred_element_type=jnp.float32,
        ).astype(jnp.bfloat16)
        return carry

    lax.fori_loop(0, cols // BLOCK, input_tile, 0)

    def own_sum(k, carry):
        facc[pl.ds(pl.multiple_of(k * r_rows, r_rows), r_rows), :] = partial_sum(z, k)
        return carry

    lax.fori_loop(0, K, own_sum, 0)

    def fin_copy(k, m):
        return remote(
            facc.at[pl.ds(pl.multiple_of(k * r_rows, r_rows), r_rows), :],
            gsib.at[pl.ds(pl.multiple_of(m * r_rows, r_rows), r_rows), :],
            fin_send.at[m], fin_recv.at[m], sibling,
        )

    near[0] = jnp.zeros(near.shape[1:], jnp.float32)

    def finish(k, carry):
        at = pl.ds(pl.multiple_of(k * r_rows, r_rows), r_rows)
        for way in (0, 1):
            p = places[way]

            @pl.when(p > 0)
            def _():
                ref = sum_chunk(way, p, k)
                line_copy(way, ref, (Z - 1) * K + k).wait_recv()
                facc[at, :] += ref[...].astype(jnp.float32)

        core = lax.div(k, K // 2)

        @pl.when(core != c)
        def _():
            fin_copy(k, k - core * (K // 2)).start()

        value = facc[at, :]
        squares = value * value
        total = squares[0:8, :]
        for i in range(1, r_rows // 8):
            total = total + squares[i * 8:(i + 1) * 8, :]
        short = total[:, 0:128]
        for i in range(1, half // 128):
            short = short + total[:, i * 128:(i + 1) * 128]
        near[0] += short
        return carry

    lax.fori_loop(0, K, finish, 0)

    for j in range(1, 2 * G):
        remote(near.at[0], near.at[j], near_send.at[j - 1], near_recv.at[j - 1], plane(j)).start()
    for j in range(1, 2 * G):
        remote(near.at[0], near.at[j], near_send.at[j - 1], near_recv.at[j - 1], plane(j)).wait_recv()
    total = near[0]
    for j in range(1, 2 * G):
        total = total + near[j]
    far[0] = total
    for j in range(1, Z):
        remote(far.at[0], far.at[j], far_send.at[j - 1], far_recv.at[j - 1], line(j)).start()
    for j in range(1, Z):
        remote(far.at[0], far.at[j], far_send.at[j - 1], far_recv.at[j - 1], line(j)).wait_recv()
    total = far[0]
    for j in range(1, Z):
        total = total + far[j]
    square_total = jnp.sum(total, axis=(0, 1), keepdims=True)
    factor = jnp.minimum(1.0, CLIP / (jnp.sqrt(square_total) + EPS_NORM))

    g_ref[:, pl.ds(pl.multiple_of(c * half, half), half)] = (
        facc[pl.ds(pl.multiple_of(c * feat, feat), feat), :] * factor)
    for m in range(K // 2):
        fin_copy(m, m).wait_recv()
    g_ref[:, pl.ds(pl.multiple_of((1 - c) * half, half), half)] = gsib[...] * factor

    for j in range(1, G):
        cot_copy(j, g).wait_send()
    for j in range(G):
        cot_pass(j, c).wait_send()
    li_copy(c, 1 - c).wait_send()

    def sent(i, carry):
        zz = lax.div(i, K)
        sib_copy(zz, c, i - zz * K).wait_send()
        return carry

    lax.fori_loop(0, Z * K, sent, 0)
    for way in (0, 1):
        @pl.when(places[way] < Z - 1)
        def _():
            for step in range(Z * K - DEPTH, Z * K):
                line_copy(way, weight_chunk(z, c, 0), step).wait_send()
    for m in range(K // 2):
        fin_copy(m, m).wait_send()
    for j in range(1, 2 * G):
        remote(near.at[0], near.at[j], near_send.at[j - 1], near_recv.at[j - 1], plane(j)).wait_send()
    for j in range(1, Z):
        remote(far.at[0], far.at[j], far_send.at[j - 1], far_recv.at[j - 1], line(j)).wait_send()


def fused(Z, G, layer_input, kv_cotangent, weight_codes, block_scales, master, moment_one, moment_two):
    tok, head = kv_cotangent.shape
    feat, cols = weight_codes.shape
    half = cols // 2
    K = PIECES
    dma = pltpu.SemaphoreType.DMA
    vmem = pl.BlockSpec(memory_space=pltpu.VMEM)
    whole = pl.BlockSpec(memory_space=pl.ANY)
    grad_input, clipped = pl.pallas_call(
        functools.partial(kernel, Z, G),
        out_shape=(
            jax.ShapeDtypeStruct((tok, cols), jnp.bfloat16),
            jax.ShapeDtypeStruct((feat, cols), jnp.float32),
        ),
        in_specs=[whole] * 4,
        out_specs=(vmem, vmem),
        scratch_shapes=[
            pltpu.VMEM((feat, cols), jnp.bfloat16),
            pltpu.VMEM((cols // BLOCK, feat), jnp.bfloat16),
            pltpu.VMEM((2 * tok, G * head), jnp.bfloat16),
            pltpu.VMEM((2 * tok, half), jnp.bfloat16),
            pltpu.VMEM((2 * Z * feat, cols), jnp.bfloat16),
            pltpu.VMEM((2, Z - 1, 2 * feat, half), jnp.bfloat16),
            pltpu.VMEM((2 * feat, half), jnp.float32),
            pltpu.VMEM((feat, half), jnp.float32),
            pltpu.VMEM((2 * G, 8, 128), jnp.float32),
            pltpu.VMEM((Z, 8, 128), jnp.float32),
            dma((4,)),
            dma((2, Z * K)), dma((2, Z * K)),
            dma((Z * K,)), dma((Z * K,)),
            dma((G - 1,)), dma((G - 1,)),
            dma((G,)), dma((G,)),
            dma((1,)), dma((1,)),
            dma((K // 2,)), dma((K // 2,)),
            dma((2 * G - 1,)), dma((2 * G - 1,)),
            dma((Z - 1,)), dma((Z - 1,)),
        ],
        compiler_params=pltpu.CompilerParams(
            collective_id=0, has_side_effects=True, vmem_limit_bytes=48 * 1024 * 1024,
        ),
        cost_estimate=pl.CostEstimate(
            flops=4 * tok * G * head * cols, bytes_accessed=10 * tok * cols, transcendentals=0,
        ),
    )(*(
        pltpu.with_memory_space_constraint(x, pltpu.HBM)
        for x in (kv_cotangent, layer_input, weight_codes, block_scales.T)
    ))
    return (grad_input,) + adamw(clipped, master, moment_one, moment_two)


def solution(mesh):
    devices, groups = mesh.shape["dp"], mesh.shape["group"]

    def shards(*args):
        tok, head = args[1].shape
        feat, cols = args[2].shape
        if devices == 8 and groups == 4 and feat == 256 and tok == 256 and cols % 512 == 0 and head == 2 * feat:
            return fused(devices // 2, groups, *args)
        return general(*args)

    return jax.shard_map(
        shards,
        mesh=mesh,
        in_specs=(P("dp", "group"),) * 7,
        out_specs=(P("dp", "group"), P("dp", "group"), P("dp", "group"), P("dp", "group")),
        check_vma=False,
    )
```

```python
import functools
import jax
import jax.numpy as jnp
from jax import lax
from jax.experimental import pallas as pl
from jax.experimental.pallas import tpu as pltpu
from jax.sharding import PartitionSpec as P

BLOCK = 256
CLIP = 2048


BETA_ONE = 0.9
BETA_TWO = 0.95
LEARN_RATE = 0.25
DECAY_RATE = 0.1
EPS_ADAM = 1e-08
EPS_NORM = 1e-06

MESH = pl.DeviceIdType.MESH
PIECES = 8
SIDES = 2
DEPTH = 5


def dequantize(codes, scales):
    row_count, col_count = codes.shape
    blocked = (
        codes.astype(jnp.float32).reshape(row_count, col_count // BLOCK, BLOCK)
        * scales.astype(jnp.float32)[:, :, None]
    )
    return blocked.reshape(row_count, col_count).astype(jnp.bfloat16)


def adamw(clipped, master, moment_one, moment_two):
    new_moment_one = BETA_ONE * moment_one + (1.0 - BETA_ONE) * clipped
    new_moment_two = BETA_TWO * moment_two + (1.0 - BETA_TWO) * clipped * clipped
    first_fix = 1.0 - BETA_ONE**10
    second_fix = 1.0 - BETA_TWO**10
    update = (new_moment_one * (1.0 / first_fix)) / (
        jnp.sqrt(new_moment_two * (1.0 / second_fix)) + EPS_ADAM
    )
    new_master = master - LEARN_RATE * (update + DECAY_RATE * master)
    return new_master, new_moment_one, new_moment_two


def general(layer_input, kv_cotangent, weight_codes, block_scales, master, moment_one, moment_two):
    cot_whole = lax.all_gather(kv_cotangent, "group", axis=1, tiled=True)
    weight_piece = dequantize(
        lax.all_gather(weight_codes, "dp", axis=0, tiled=True),
        lax.all_gather(block_scales, "dp", axis=0, tiled=True),
    )
    grad_input = jnp.dot(
        cot_whole, weight_piece, preferred_element_type=jnp.float32
    ).astype(jnp.bfloat16)
    partial_value = jnp.einsum(
        "tc,td->cd", cot_whole, layer_input, preferred_element_type=jnp.float32
    )
    gradient = lax.psum_scatter(
        lax.optimization_barrier(partial_value.astype(jnp.bfloat16)).astype(jnp.float32),
        "dp",
        scatter_dimension=0,
        tiled=True,
    )
    square_total = lax.psum(jnp.sum(gradient * gradient), ("dp", "group"))
    factor = jnp.minimum(1.0, CLIP / (jnp.sqrt(square_total) + EPS_NORM))
    return (grad_input,) + adamw(gradient * factor, master, moment_one, moment_two)


def kernel(
    Z, G, cot_ref, li_ref, codes_ref, scales_ref, gi_ref, g_ref,
    codes, scales_in, cotp, lip, wbuf, rbuf, facc, gsib, near, far, local,
    line_send, line_recv, sib_send, sib_recv, cot_send, cot_recv, csib_send, csib_recv,
    li_send, li_recv, fin_send, fin_recv, near_send, near_recv, far_send, far_recv,
):
    K = PIECES
    tok, head = cot_ref.shape
    feat, cols = codes_ref.shape
    half = cols // 2
    unit = 2 * feat
    g_rows, r_rows, r_cols = feat // K, unit // (K // SIDES), half // SIDES

    dp, g = lax.axis_index("dp"), lax.axis_index("group")
    z = lax.div(dp, 2)
    c = dp - 2 * z
    sibling = (2 * z + 1 - c, g)

    def plane(j):
        place = lax.rem(c * G + g + j, 2 * G)
        core = lax.div(place, G)
        return (2 * z + core, place - core * G)

    def line(j):
        return (2 * lax.rem(z + j, Z) + c, g)

    barrier = pltpu.get_barrier_semaphore()
    for j in range(1, 2 * G):
        pl.semaphore_signal(barrier, inc=1, device_id=plane(j), device_id_type=MESH)
    for j in range(1, Z):
        pl.semaphore_signal(barrier, inc=1, device_id=line(j), device_id_type=MESH)

    fetch_codes = pltpu.make_async_copy(codes_ref, codes, local.at[2])
    fetch_scales = pltpu.make_async_copy(scales_ref, scales_in, local.at[3])
    fetch_codes.start()
    fetch_scales.start()
    own_tok = pl.ds(pl.multiple_of(c * tok, tok), tok)
    fetch_li = pltpu.make_async_copy(
        li_ref.at[:, pl.ds(pl.multiple_of(c * half, half), half)], lip.at[own_tok, :], local.at[0])
    fetch_cot = pltpu.make_async_copy(
        cot_ref, cotp.at[own_tok, pl.ds(pl.multiple_of(g * head, head), head)], local.at[1])
    fetch_li.start()
    fetch_cot.start()

    own = pl.multiple_of(dp * feat, feat)
    fetch_scales.wait()
    scales = scales_in[...].astype(jnp.float32).T
    fetch_codes.wait()
    for j in range(cols // BLOCK):
        wbuf[pl.ds(own, feat), j * BLOCK:(j + 1) * BLOCK] = (
            codes[:, j * BLOCK:(j + 1) * BLOCK].astype(jnp.float32) * scales[:, j:j + 1]
        ).astype(jnp.bfloat16)

    pl.semaphore_wait(barrier, 2 * G - 1 + Z - 1)

    def remote(src, dst, send, recv, device):
        return pltpu.make_async_remote_copy(
            src_ref=src, dst_ref=dst, send_sem=send, recv_sem=recv,
            device_id=device, device_id_type=MESH,
        )

    def cot_block(owner, core):
        return cotp.at[
            pl.ds(pl.multiple_of(core * tok, tok), tok),
            pl.ds(pl.multiple_of(owner * head, head), head),
        ]

    def cot_copy(j, owner):
        return remote(cot_ref, cot_block(owner, c), cot_send.at[j - 1], cot_recv.at[j - 1],
                      (dp, lax.rem(g + j, G)))

    def cot_pass(j, core):
        owner = lax.rem(g + G - j, G)
        block = cot_block(owner, core)
        return remote(cot_ref if j == 0 else block, block, csib_send.at[j], csib_recv.at[j], sibling)

    for j in range(1, G):
        cot_copy(j, g).start()
    cot_pass(0, c).start()

    def li_copy(core, side):
        return remote(
            li_ref.at[:, pl.ds(pl.multiple_of(side * half, half), half)],
            lip.at[pl.ds(pl.multiple_of(core * tok, tok), tok), :],
            li_send.at[0], li_recv.at[0], sibling,
        )

    li_copy(c, 1 - c).start()

    places = (z, Z - 1 - z)
    nexts = ((dp + 2, g), (dp - 2, g))

    def true_z(way, q):
        return q if way == 0 else Z - 1 - q

    def weight_chunk(zz, core, k):
        return wbuf.at[pl.ds(pl.multiple_of((2 * zz + core) * feat + k * g_rows, g_rows), g_rows), :]

    def span(k):
        row = lax.div(k, SIDES)
        col = k - row * SIDES
        return (pl.ds(pl.multiple_of(row * r_rows, r_rows), r_rows),
                pl.ds(pl.multiple_of(col * r_cols, r_cols), r_cols))

    def sum_chunk(way, dm, k):
        return rbuf.at[(way, dm - 1) + span(k)]

    def line_copy(way, ref, step):
        return remote(ref, ref, line_send.at[way, step], line_recv.at[way, step], nexts[way])

    def sib_copy(zz, core, k):
        ref = weight_chunk(zz, core, k)
        return remote(ref, ref, sib_send.at[zz * K + k], sib_recv.at[zz * K + k], sibling)

    def partial_sum(zz, k):
        first = pl.multiple_of(zz * unit + lax.div(k, SIDES) * r_rows, r_rows)
        return lax.dot_general(
            cotp[:, pl.ds(first, r_rows)], lip[:, span(k)[1]],
            (((0,), (0,)), ((), ())), preferred_element_type=jnp.float32,
        )

    def send(way, ref, step):
        @pl.when(step >= DEPTH)
        def _():
            line_copy(way, weight_chunk(z, c, 0), step - DEPTH).wait_send()
        line_copy(way, ref, step).start()

    def weight_step(way, s, k):
        p = places[way]

        @pl.when(s <= p)
        def _():
            zz = true_z(way, p - s)
            ref = weight_chunk(zz, c, k)

            @pl.when(s > 0)
            def _():
                line_copy(way, ref, (s - 1) * K + k).wait_recv()

            @pl.when((s > 0) if way else (s >= 0))
            def _():
                sib_copy(zz, c, k).start()

            @pl.when(p < Z - 1)
            def _():
                send(way, ref, s * K + k)

    def sum_step(way, s, k):
        p = places[way]

        @pl.when((s > p) & (p < Z - 1))
        def _():
            dm = Z + p - s
            ref = sum_chunk(way, dm, k)
            value = partial_sum(true_z(way, dm), k)

            @pl.when(p > 0)
            def _():
                line_copy(way, ref, (s - 1) * K + k).wait_recv()
                ref[...] = (ref[...].astype(jnp.float32) + value).astype(jnp.bfloat16)

            @pl.when(p == 0)
            def _():
                ref[...] = value.astype(jnp.bfloat16)

            send(way, ref, s * K + k)

    def first_unit(k, carry):
        for way in (0, 1):
            weight_step(way, 0, k)
        return carry

    lax.fori_loop(0, DEPTH, first_unit, 0)
    for j in range(1, G):
        cot_copy(j, lax.rem(g + G - j, G)).wait_recv()
        cot_pass(j, c).start()
    lax.fori_loop(DEPTH, K, first_unit, 0)
    fetch_li.wait()
    fetch_cot.wait()
    li_copy(1 - c, c).wait_recv()
    for j in range(G):
        cot_pass(j, 1 - c).wait_recv()

    def later_unit(i, carry):
        s = lax.div(i, K)
        k = i - s * K
        for way in (0, 1):
            weight_step(way, s, k)
        for way in (0, 1):
            sum_step(way, s, k)
        return carry

    lax.fori_loop(K, Z * K, later_unit, 0)

    def arrive(i, carry):
        zz = lax.div(i, K)
        sib_copy(zz, 1 - c, i - zz * K).wait_recv()
        return carry

    lax.fori_loop(0, Z * K, arrive, 0)

    def input_tile(j, carry):
        at = pl.ds(pl.multiple_of(j * BLOCK, BLOCK), BLOCK)
        gi_ref[:, at] = jnp.dot(
            cotp[pl.ds(pl.multiple_of(c * tok, tok), tok), :], wbuf[:, at],
            preferred_element_type=jnp.float32,
        ).astype(jnp.bfloat16)
        return carry

    lax.fori_loop(0, cols // BLOCK, input_tile, 0)

    def own_sum(k, carry):
        facc[span(k)] = partial_sum(z, k)
        return carry

    lax.fori_loop(0, K, own_sum, 0)

    def fin_copy(k, m):
        return remote(
            facc.at[span(k)], gsib.at[span(m)],
            fin_send.at[m], fin_recv.at[m], sibling,
        )

    near[0] = jnp.zeros(near.shape[1:], jnp.float32)

    def finish(k, carry):
        at = span(k)
        for way in (0, 1):
            p = places[way]

            @pl.when(p > 0)
            def _():
                ref = sum_chunk(way, p, k)
                line_copy(way, ref, (Z - 1) * K + k).wait_recv()
                facc[at] += ref[...].astype(jnp.float32)

        core = lax.div(k, K // 2)

        @pl.when(core != c)
        def _():
            fin_copy(k, k - core * (K // 2)).start()

        value = facc[at]
        squares = value * value
        total = squares[0:8, :]
        for i in range(1, r_rows // 8):
            total = total + squares[i * 8:(i + 1) * 8, :]
        short = total[:, 0:128]
        for i in range(1, r_cols // 128):
            short = short + total[:, i * 128:(i + 1) * 128]
        near[0] += short
        return carry

    lax.fori_loop(0, K, finish, 0)

    for j in range(1, 2 * G):
        remote(near.at[0], near.at[j], near_send.at[j - 1], near_recv.at[j - 1], plane(j)).start()
    for j in range(1, 2 * G):
        remote(near.at[0], near.at[j], near_send.at[j - 1], near_recv.at[j - 1], plane(j)).wait_recv()
    total = near[0]
    for j in range(1, 2 * G):
        total = total + near[j]
    far[0] = total
    for j in range(1, Z):
        remote(far.at[0], far.at[j], far_send.at[j - 1], far_recv.at[j - 1], line(j)).start()
    for j in range(1, Z):
        remote(far.at[0], far.at[j], far_send.at[j - 1], far_recv.at[j - 1], line(j)).wait_recv()
    total = far[0]
    for j in range(1, Z):
        total = total + far[j]
    square_total = jnp.sum(total, axis=(0, 1), keepdims=True)
    factor = jnp.minimum(1.0, CLIP / (jnp.sqrt(square_total) + EPS_NORM))

    g_ref[:, pl.ds(pl.multiple_of(c * half, half), half)] = (
        facc[pl.ds(pl.multiple_of(c * feat, feat), feat), :] * factor)
    for m in range(K // 2):
        fin_copy(m, m).wait_recv()
    g_ref[:, pl.ds(pl.multiple_of((1 - c) * half, half), half)] = gsib[...] * factor

    for j in range(1, G):
        cot_copy(j, g).wait_send()
    for j in range(G):
        cot_pass(j, c).wait_send()
    li_copy(c, 1 - c).wait_send()

    def sent(i, carry):
        zz = lax.div(i, K)
        sib_copy(zz, c, i - zz * K).wait_send()
        return carry

    lax.fori_loop(0, Z * K, sent, 0)
    for way in (0, 1):
        @pl.when(places[way] < Z - 1)
        def _():
            for step in range(Z * K - DEPTH, Z * K):
                line_copy(way, weight_chunk(z, c, 0), step).wait_send()
    for m in range(K // 2):
        fin_copy(m, m).wait_send()
    for j in range(1, 2 * G):
        remote(near.at[0], near.at[j], near_send.at[j - 1], near_recv.at[j - 1], plane(j)).wait_send()
    for j in range(1, Z):
        remote(far.at[0], far.at[j], far_send.at[j - 1], far_recv.at[j - 1], line(j)).wait_send()


def fused(Z, G, layer_input, kv_cotangent, weight_codes, block_scales, master, moment_one, moment_two):
    tok, head = kv_cotangent.shape
    feat, cols = weight_codes.shape
    half = cols // 2
    K = PIECES
    dma = pltpu.SemaphoreType.DMA
    vmem = pl.BlockSpec(memory_space=pltpu.VMEM)
    whole = pl.BlockSpec(memory_space=pl.ANY)
    grad_input, clipped = pl.pallas_call(
        functools.partial(kernel, Z, G),
        out_shape=(
            jax.ShapeDtypeStruct((tok, cols), jnp.bfloat16),
            jax.ShapeDtypeStruct((feat, cols), jnp.float32),
        ),
        in_specs=[whole] * 4,
        out_specs=(vmem, vmem),
        scratch_shapes=[
            pltpu.VMEM((feat, cols), jnp.bfloat16),
            pltpu.VMEM((cols // BLOCK, feat), jnp.bfloat16),
            pltpu.VMEM((2 * tok, G * head), jnp.bfloat16),
            pltpu.VMEM((2 * tok, half), jnp.bfloat16),
            pltpu.VMEM((2 * Z * feat, cols), jnp.bfloat16),
            pltpu.VMEM((2, Z - 1, 2 * feat, half), jnp.bfloat16),
            pltpu.VMEM((2 * feat, half), jnp.float32),
            pltpu.VMEM((feat, half), jnp.float32),
            pltpu.VMEM((2 * G, 8, 128), jnp.float32),
            pltpu.VMEM((Z, 8, 128), jnp.float32),
            dma((4,)),
            dma((2, Z * K)), dma((2, Z * K)),
            dma((Z * K,)), dma((Z * K,)),
            dma((G - 1,)), dma((G - 1,)),
            dma((G,)), dma((G,)),
            dma((1,)), dma((1,)),
            dma((K // 2,)), dma((K // 2,)),
            dma((2 * G - 1,)), dma((2 * G - 1,)),
            dma((Z - 1,)), dma((Z - 1,)),
        ],
        compiler_params=pltpu.CompilerParams(
            collective_id=0, has_side_effects=True, vmem_limit_bytes=48 * 1024 * 1024,
        ),
        cost_estimate=pl.CostEstimate(
            flops=4 * tok * G * head * cols, bytes_accessed=10 * tok * cols, transcendentals=0,
        ),
    )(*(
        pltpu.with_memory_space_constraint(x, pltpu.HBM)
        for x in (kv_cotangent, layer_input, weight_codes, block_scales.T)
    ))
    return (grad_input,) + adamw(clipped, master, moment_one, moment_two)


def solution(mesh):
    devices, groups = mesh.shape["dp"], mesh.shape["group"]

    def shards(*args):
        tok, head = args[1].shape
        feat, cols = args[2].shape
        if devices == 8 and groups == 4 and feat == 256 and tok == 256 and cols % 512 == 0 and head == 2 * feat:
            return fused(devices // 2, groups, *args)
        return general(*args)

    return jax.shard_map(
        shards,
        mesh=mesh,
        in_specs=(P("dp", "group"),) * 7,
        out_specs=(P("dp", "group"), P("dp", "group"), P("dp", "group"), P("dp", "group")),
        check_vma=False,
    )
```

```python
import functools
import jax
import jax.numpy as jnp
from jax import lax
from jax.experimental import pallas as pl
from jax.experimental.pallas import tpu as pltpu
from jax.sharding import PartitionSpec as P

BLOCK = 256
CLIP = 2048


BETA_ONE = 0.9
BETA_TWO = 0.95
LEARN_RATE = 0.25
DECAY_RATE = 0.1
EPS_ADAM = 1e-08
EPS_NORM = 1e-06

MESH = pl.DeviceIdType.MESH
PIECES = 4
DEPTH = 2


def dequantize(codes, scales):
    row_count, col_count = codes.shape
    blocked = (
        codes.astype(jnp.float32).reshape(row_count, col_count // BLOCK, BLOCK)
        * scales.astype(jnp.float32)[:, :, None]
    )
    return blocked.reshape(row_count, col_count).astype(jnp.bfloat16)


def adamw(clipped, master, moment_one, moment_two):
    new_moment_one = BETA_ONE * moment_one + (1.0 - BETA_ONE) * clipped
    new_moment_two = BETA_TWO * moment_two + (1.0 - BETA_TWO) * clipped * clipped
    first_fix = 1.0 - BETA_ONE**10
    second_fix = 1.0 - BETA_TWO**10
    update = new_moment_one / first_fix / (jnp.sqrt(new_moment_two / second_fix) + EPS_ADAM)
    new_master = master - LEARN_RATE * (update + DECAY_RATE * master)
    return new_master, new_moment_one, new_moment_two


def general(layer_input, kv_cotangent, weight_codes, block_scales, master, moment_one, moment_two):
    cot_whole = lax.all_gather(kv_cotangent, "group", axis=1, tiled=True)
    weight_piece = dequantize(
        lax.all_gather(weight_codes, "dp", axis=0, tiled=True),
        lax.all_gather(block_scales, "dp", axis=0, tiled=True),
    )
    grad_input = jnp.dot(
        cot_whole, weight_piece, preferred_element_type=jnp.float32
    ).astype(jnp.bfloat16)
    partial_value = jnp.einsum(
        "tc,td->cd", cot_whole, layer_input, preferred_element_type=jnp.float32
    )
    gradient = lax.psum_scatter(
        lax.optimization_barrier(partial_value.astype(jnp.bfloat16)).astype(jnp.float32),
        "dp",
        scatter_dimension=0,
        tiled=True,
    )
    square_total = lax.psum(jnp.sum(gradient * gradient), ("dp", "group"))
    factor = jnp.minimum(1.0, CLIP / (jnp.sqrt(square_total) + EPS_NORM))
    return (grad_input,) + adamw(gradient * factor, master, moment_one, moment_two)


def kernel(
    Z, G, cot_ref, li_ref, codes_ref, scales_ref, gi_ref, g_ref,
    codes, scales_in, cotp, lip, wbuf, rbuf, facc, gsib, near, far, local,
    line_send, line_recv, sib_send, sib_recv, cot_send, cot_recv, csib_send, csib_recv,
    li_send, li_recv, fin_send, fin_recv, near_send, near_recv, far_send, far_recv,
):
    K = PIECES
    tok, head = cot_ref.shape
    feat, cols = codes_ref.shape
    half = cols // 2
    unit = 2 * feat
    g_rows, r_rows = feat // K, unit // K

    dp, g = lax.axis_index("dp"), lax.axis_index("group")
    z = lax.div(dp, 2)
    c = dp - 2 * z
    sibling = (2 * z + 1 - c, g)

    def plane(j):
        place = lax.rem(c * G + g + j, 2 * G)
        core = lax.div(place, G)
        return (2 * z + core, place - core * G)

    def line(j):
        return (2 * lax.rem(z + j, Z) + c, g)

    barrier = pltpu.get_barrier_semaphore()
    for j in range(1, 2 * G):
        pl.semaphore_signal(barrier, inc=1, device_id=plane(j), device_id_type=MESH)
    for j in range(1, Z):
        pl.semaphore_signal(barrier, inc=1, device_id=line(j), device_id_type=MESH)

    fetch_codes = pltpu.make_async_copy(codes_ref, codes, local.at[2])
    fetch_scales = pltpu.make_async_copy(scales_ref, scales_in, local.at[3])
    fetch_codes.start()
    fetch_scales.start()
    own_tok = pl.ds(pl.multiple_of(c * tok, tok), tok)
    fetch_li = pltpu.make_async_copy(
        li_ref.at[:, pl.ds(pl.multiple_of(c * half, half), half)], lip.at[own_tok, :], local.at[0])
    fetch_cot = pltpu.make_async_copy(
        cot_ref, cotp.at[own_tok, pl.ds(pl.multiple_of(g * head, head), head)], local.at[1])
    fetch_li.start()
    fetch_cot.start()

    own = pl.multiple_of(dp * feat, feat)
    fetch_scales.wait()
    scales = scales_in[...].astype(jnp.float32).T
    fetch_codes.wait()
    for j in range(cols // BLOCK):
        wbuf[pl.ds(own, feat), j * BLOCK:(j + 1) * BLOCK] = (
            codes[:, j * BLOCK:(j + 1) * BLOCK].astype(jnp.float32) * scales[:, j:j + 1]
        ).astype(jnp.bfloat16)

    pl.semaphore_wait(barrier, 2 * G - 1 + Z - 1)

    def remote(src, dst, send, recv, device):
        return pltpu.make_async_remote_copy(
            src_ref=src, dst_ref=dst, send_sem=send, recv_sem=recv,
            device_id=device, device_id_type=MESH,
        )

    def cot_block(owner, core):
        return cotp.at[
            pl.ds(pl.multiple_of(core * tok, tok), tok),
            pl.ds(pl.multiple_of(owner * head, head), head),
        ]

    def cot_copy(j, owner):
        return remote(cot_ref, cot_block(owner, c), cot_send.at[j - 1], cot_recv.at[j - 1],
                      (dp, lax.rem(g + j, G)))

    def cot_pass(j, core):
        owner = lax.rem(g + G - j, G)
        block = cot_block(owner, core)
        return remote(cot_ref if j == 0 else block, block, csib_send.at[j], csib_recv.at[j], sibling)

    for j in range(1, G):
        cot_copy(j, g).start()
    cot_pass(0, c).start()

    def li_copy(core, side):
        return remote(
            li_ref.at[:, pl.ds(pl.multiple_of(side * half, half), half)],
            lip.at[pl.ds(pl.multiple_of(core * tok, tok), tok), :],
            li_send.at[0], li_recv.at[0], sibling,
        )

    li_copy(c, 1 - c).start()

    places = (z, Z - 1 - z)
    nexts = ((dp + 2, g), (dp - 2, g))

    def true_z(way, q):
        return q if way == 0 else Z - 1 - q

    def weight_chunk(zz, core, k):
        return wbuf.at[pl.ds(pl.multiple_of((2 * zz + core) * feat + k * g_rows, g_rows), g_rows), :]

    def sum_chunk(way, dm, k):
        return rbuf.at[way, dm - 1, pl.ds(pl.multiple_of(k * r_rows, r_rows), r_rows), :]

    def line_copy(way, ref, step):
        return remote(ref, ref, line_send.at[way, step], line_recv.at[way, step], nexts[way])

    def sib_copy(zz, core, k):
        ref = weight_chunk(zz, core, k)
        return remote(ref, ref, sib_send.at[zz * K + k], sib_recv.at[zz * K + k], sibling)

    def partial_sum(zz, k):
        first = pl.multiple_of(zz * unit + k * r_rows, r_rows)
        return lax.dot_general(
            cotp[:, pl.ds(first, r_rows)], lip[...],
            (((0,), (0,)), ((), ())), preferred_element_type=jnp.float32,
        )

    def send(way, ref, step):
        @pl.when(step >= DEPTH)
        def _():
            line_copy(way, weight_chunk(z, c, 0), step - DEPTH).wait_send()
        line_copy(way, ref, step).start()

    def weight_step(way, s, k):
        p = places[way]

        @pl.when(s <= p)
        def _():
            zz = true_z(way, p - s)
            ref = weight_chunk(zz, c, k)

            @pl.when(s > 0)
            def _():
                line_copy(way, ref, (s - 1) * K + k).wait_recv()

            @pl.when((s > 0) if way else (s >= 0))
            def _():
                sib_copy(zz, c, k).start()

            @pl.when(p < Z - 1)
            def _():
                send(way, ref, s * K + k)

    def sum_step(way, s, k):
        p = places[way]

        @pl.when((s > p) & (p < Z - 1))
        def _():
            dm = Z + p - s
            ref = sum_chunk(way, dm, k)
            value = partial_sum(true_z(way, dm), k)

            @pl.when(p > 0)
            def _():
                line_copy(way, ref, (s - 1) * K + k).wait_recv()
                ref[...] = (ref[...].astype(jnp.float32) + value).astype(jnp.bfloat16)

            @pl.when(p == 0)
            def _():
                ref[...] = value.astype(jnp.bfloat16)

            send(way, ref, s * K + k)

    def first_unit(k, carry):
        for way in (0, 1):
            weight_step(way, 0, k)
        return carry

    lax.fori_loop(0, DEPTH, first_unit, 0)
    for j in range(1, G):
        cot_copy(j, lax.rem(g + G - j, G)).wait_recv()
        cot_pass(j, c).start()
    lax.fori_loop(DEPTH, K, first_unit, 0)
    fetch_li.wait()
    fetch_cot.wait()
    li_copy(1 - c, c).wait_recv()
    for j in range(G):
        cot_pass(j, 1 - c).wait_recv()

    def later_unit(i, carry):
        s = lax.div(i, K)
        k = i - s * K
        for way in (0, 1):
            weight_step(way, s, k)
        for way in (0, 1):
            sum_step(way, s, k)
        return carry

    lax.fori_loop(K, Z * K, later_unit, 0)

    def arrive(i, carry):
        zz = lax.div(i, K)
        sib_copy(zz, 1 - c, i - zz * K).wait_recv()
        return carry

    lax.fori_loop(0, Z * K, arrive, 0)

    def input_tile(j, carry):
        at = pl.ds(pl.multiple_of(j * BLOCK, BLOCK), BLOCK)
        gi_ref[:, at] = jnp.dot(
            cotp[pl.ds(pl.multiple_of(c * tok, tok), tok), :], wbuf[:, at],
            preferred_element_type=jnp.float32,
        ).astype(jnp.bfloat16)
        return carry

    lax.fori_loop(0, cols // BLOCK, input_tile, 0)

    def own_sum(k, carry):
        facc[pl.ds(pl.multiple_of(k * r_rows, r_rows), r_rows), :] = partial_sum(z, k)
        return carry

    lax.fori_loop(0, K, own_sum, 0)

    def fin_copy(k, m):
        return remote(
            facc.at[pl.ds(pl.multiple_of(k * r_rows, r_rows), r_rows), :],
            gsib.at[pl.ds(pl.multiple_of(m * r_rows, r_rows), r_rows), :],
            fin_send.at[m], fin_recv.at[m], sibling,
        )

    near[0] = jnp.zeros(near.shape[1:], jnp.float32)

    def finish(k, carry):
        at = pl.ds(pl.multiple_of(k * r_rows, r_rows), r_rows)
        for way in (0, 1):
            p = places[way]

            @pl.when(p > 0)
            def _():
                ref = sum_chunk(way, p, k)
                line_copy(way, ref, (Z - 1) * K + k).wait_recv()
                facc[at, :] += ref[...].astype(jnp.float32)

        core = lax.div(k, K // 2)

        @pl.when(core != c)
        def _():
            fin_copy(k, k - core * (K // 2)).start()

        value = facc[at, :]
        squares = value * value
        total = squares[0:8, :]
        for i in range(1, r_rows // 8):
            total = total + squares[i * 8:(i + 1) * 8, :]
        short = total[:, 0:128]
        for i in range(1, half // 128):
            short = short + total[:, i * 128:(i + 1) * 128]
        near[0] += short
        return carry

    lax.fori_loop(0, K, finish, 0)

    for j in range(1, 2 * G):
        remote(near.at[0], near.at[j], near_send.at[j - 1], near_recv.at[j - 1], plane(j)).start()
    for j in range(1, 2 * G):
        remote(near.at[0], near.at[j], near_send.at[j - 1], near_recv.at[j - 1], plane(j)).wait_recv()
    total = near[0]
    for j in range(1, 2 * G):
        total = total + near[j]
    far[0] = total
    for j in range(1, Z):
        remote(far.at[0], far.at[j], far_send.at[j - 1], far_recv.at[j - 1], line(j)).start()
    for j in range(1, Z):
        remote(far.at[0], far.at[j], far_send.at[j - 1], far_recv.at[j - 1], line(j)).wait_recv()
    total = far[0]
    for j in range(1, Z):
        total = total + far[j]
    square_total = jnp.sum(total, axis=(0, 1), keepdims=True)
    factor = jnp.minimum(1.0, CLIP / (jnp.sqrt(square_total) + EPS_NORM))

    g_ref[:, pl.ds(pl.multiple_of(c * half, half), half)] = (
        facc[pl.ds(pl.multiple_of(c * feat, feat), feat), :] * factor)
    for m in range(K // 2):
        fin_copy(m, m).wait_recv()
    g_ref[:, pl.ds(pl.multiple_of((1 - c) * half, half), half)] = gsib[...] * factor

    for j in range(1, G):
        cot_copy(j, g).wait_send()
    for j in range(G):
        cot_pass(j, c).wait_send()
    li_copy(c, 1 - c).wait_send()

    def sent(i, carry):
        zz = lax.div(i, K)
        sib_copy(zz, c, i - zz * K).wait_send()
        return carry

    lax.fori_loop(0, Z * K, sent, 0)
    for way in (0, 1):
        @pl.when(places[way] < Z - 1)
        def _():
            for step in range(Z * K - DEPTH, Z * K):
                line_copy(way, weight_chunk(z, c, 0), step).wait_send()
    for m in range(K // 2):
        fin_copy(m, m).wait_send()
    for j in range(1, 2 * G):
        remote(near.at[0], near.at[j], near_send.at[j - 1], near_recv.at[j - 1], plane(j)).wait_send()
    for j in range(1, Z):
        remote(far.at[0], far.at[j], far_send.at[j - 1], far_recv.at[j - 1], line(j)).wait_send()


def fused(Z, G, layer_input, kv_cotangent, weight_codes, block_scales, master, moment_one, moment_two):
    tok, head = kv_cotangent.shape
    feat, cols = weight_codes.shape
    half = cols // 2
    K = PIECES
    dma = pltpu.SemaphoreType.DMA
    vmem = pl.BlockSpec(memory_space=pltpu.VMEM)
    whole = pl.BlockSpec(memory_space=pl.ANY)
    grad_input, clipped = pl.pallas_call(
        functools.partial(kernel, Z, G),
        out_shape=(
            jax.ShapeDtypeStruct((tok, cols), jnp.bfloat16),
            jax.ShapeDtypeStruct((feat, cols), jnp.float32),
        ),
        in_specs=[whole] * 4,
        out_specs=(vmem, vmem),
        scratch_shapes=[
            pltpu.VMEM((feat, cols), jnp.bfloat16),
            pltpu.VMEM((cols // BLOCK, feat), jnp.bfloat16),
            pltpu.VMEM((2 * tok, G * head), jnp.bfloat16),
            pltpu.VMEM((2 * tok, half), jnp.bfloat16),
            pltpu.VMEM((2 * Z * feat, cols), jnp.bfloat16),
            pltpu.VMEM((2, Z - 1, 2 * feat, half), jnp.bfloat16),
            pltpu.VMEM((2 * feat, half), jnp.float32),
            pltpu.VMEM((feat, half), jnp.float32),
            pltpu.VMEM((2 * G, 8, 128), jnp.float32),
            pltpu.VMEM((Z, 8, 128), jnp.float32),
            dma((4,)),
            dma((2, Z * K)), dma((2, Z * K)),
            dma((Z * K,)), dma((Z * K,)),
            dma((G - 1,)), dma((G - 1,)),
            dma((G,)), dma((G,)),
            dma((1,)), dma((1,)),
            dma((K // 2,)), dma((K // 2,)),
            dma((2 * G - 1,)), dma((2 * G - 1,)),
            dma((Z - 1,)), dma((Z - 1,)),
        ],
        compiler_params=pltpu.CompilerParams(
            collective_id=0, has_side_effects=True, vmem_limit_bytes=48 * 1024 * 1024,
        ),
        cost_estimate=pl.CostEstimate(
            flops=4 * tok * G * head * cols, bytes_accessed=10 * tok * cols, transcendentals=0,
        ),
    )(*(
        pltpu.with_memory_space_constraint(x, pltpu.HBM)
        for x in (kv_cotangent, layer_input, weight_codes, block_scales.T)
    ))
    return (grad_input,) + adamw(clipped, master, moment_one, moment_two)


def solution(mesh):
    devices, groups = mesh.shape["dp"], mesh.shape["group"]

    def shards(*args):
        tok, head = args[1].shape
        feat, cols = args[2].shape
        if devices == 8 and groups == 4 and feat == 256 and tok == 256 and cols % 512 == 0 and head == 2 * feat:
            return fused(devices // 2, groups, *args)
        return general(*args)

    return jax.shard_map(
        shards,
        mesh=mesh,
        in_specs=(P("dp", "group"),) * 7,
        out_specs=(P("dp", "group"), P("dp", "group"), P("dp", "group"), P("dp", "group")),
        check_vma=False,
    )
```
